32 devices in a mesh: req: 8 (over z, x), kv: 4 (over y, core).
Axes of the slice: x: 2, y: 2, z: 4, core: 2. Of those that a mesh axis runs over, the one named last changes fastest.
Arguments:
- residual_in: bfloat16 [16, 2560], P('req', 'kv'), may hold values from -8 to 8
- queries: bfloat16 [16, 2560], P('req', 'kv'), may hold values from -480 to 480
- fresh_token_keys: bfloat16 [16, 512], P('req', 'kv'), may hold values from -6 to 6
- fresh_token_values: bfloat16 [16, 512], P('req', 'kv'), may hold values from -6 to 6
- cached_key_slots: bfloat16 [16, 4096, 512], P('req', None, 'kv'), may hold values from -6 to 6
- cached_value_slots: bfloat16 [16, 4096, 512], P('req', None, 'kv'), may hold values from -6 to 6
- lengths: int32 [16], replicated, may hold values from 1 to 4096, as said below
- slot_order: int32 [16], replicated, may hold values from 0 to 15, as said below
- out_proj: bfloat16 [2560, 2560], P('kv'), may hold values from -0.5 to 0.5
- norm_gain: bfloat16 [2560], P('kv'), may hold values from 0.5 to 1.5
- expert_ids: int32 [16, 6], replicated, may hold values from 0 to 7, all different within a row; in each aligned block of 16 rows (0 to 15, 16 to 31, ...) at most 16 rows name the same one
- gate_values: float32 [16, 6], replicated, may hold values from 0.1 to 0.5
- gate_proj: bfloat16 [8, 2560, 1536], P('req', None, 'kv'), may hold values from -0.125 to 0.125
- up_proj: bfloat16 [8, 2560, 1536], P('req', None, 'kv'), may hold values from -0.125 to 0.125
- down_proj: bfloat16 [8, 1536, 2560], P('req', 'kv'), may hold values from -0.15625 to 0.15625
Outputs:
- layer_out: bfloat16 [16, 2560], P('req', 'kv')
The draws below stay inside these ranges and needn't reach their ends.
Inputs may be any that keep to these rules, and one draw needn't show every extreme that they name: `lengths`: each request's count of cached positions; some request has exactly 4096. A permutation of the requests: slot s serves request slot_order[s], and cached_key_slots[s], cached_value_slots[s] hold that request's cache. Requests sorted by decreasing length are dealt to the 8 groups of 2 consecutive slots, one round forward, the next backward. `expert_ids`: each token names 6 different experts; no expert is named by more than 16 tokens, a bound that some block reaches.
All inputs are finite; a program needn't handle non-finite values.
Results may differ from the reference program's by a relative error of at most 0.012.
Values may be sent and summed in bfloat16 or wider, within the bound.
A program may use at most 64 MiB of HBM per device.

```python
import math
import jax
import jax.numpy as jnp
import numpy as np
from jax import lax

D = 2560
QUERY_HEADS = 20
KEY_VALUE_HEADS = 4
HEAD_SIZE = 128
FE = 1536
TOPK = 6
REQ_DEV = 2
LONGEST_LENGTH = 4096
REQUEST_TOTAL = 16
NE = 8
CAPE = 16


def length_table(key):
    base_key = jax.random.fold_in(key, 11)
    first_key = jax.random.fold_in(base_key, 1)
    second_key = jax.random.fold_in(base_key, 2)
    third_key = jax.random.fold_in(base_key, 3)
    ceiling = jax.random.randint(first_key, (REQUEST_TOTAL,), 1, LONGEST_LENGTH + 1)
    raw_len = jax.random.randint(second_key, (REQUEST_TOTAL,), 0, LONGEST_LENGTH)
    lens_all = 1 + raw_len % ceiling
    spot_row = jax.random.randint(third_key, (), 0, REQUEST_TOTAL)
    return jnp.where(jnp.arange(REQUEST_TOTAL) == spot_row, LONGEST_LENGTH, lens_all).astype(jnp.int32)


def draw_lengths(key, part):
    return length_table(key)


def draw_slot_order(key, part):
    lens_all = length_table(key)
    ranking = lens_all * REQUEST_TOTAL + jnp.arange(REQUEST_TOTAL, dtype=jnp.int32)
    sorted_req = jnp.argsort(-ranking, stable=True).astype(jnp.int32)
    groups = REQUEST_TOTAL // REQ_DEV
    slot_ids = jnp.arange(REQUEST_TOTAL, dtype=jnp.int32)
    group_id = slot_ids // REQ_DEV
    round_id = slot_ids % REQ_DEV
    rank_pos = round_id * groups + jnp.where(round_id % 2 == 0, group_id, groups - 1 - group_id)
    return sorted_req[rank_pos].astype(jnp.int32)


def draw_queries(key, part):
    values = jax.random.truncated_normal(jax.random.fold_in(key, 3), -6.0, 6.0, (REQUEST_TOTAL, QUERY_HEADS, HEAD_SIZE), jnp.float32) * 2.0
    return values.reshape(REQUEST_TOTAL, QUERY_HEADS * HEAD_SIZE).astype(jnp.bfloat16)


def draw_residual_in(key, part):
    base = jax.random.truncated_normal(jax.random.fold_in(key, 21), -3.0, 3.0, (REQUEST_TOTAL, D), jnp.float32)
    place = jnp.arange(D, dtype=jnp.float32) / (D - 1)
    column_scale = 0.3 * jnp.exp(place * math.log(5.0))
    values = base * column_scale[None, :]
    return jnp.clip(values, -8.0, 8.0).astype(jnp.bfloat16)


def level_of(key, dims, split, low, top_value):
    gain, own = 1.0, jax.random.fold_in(key, 6)
    for position, shards_of in split:
        heights = jnp.exp(jax.random.uniform(jax.random.fold_in(own, position), (shards_of,), jnp.float32, low / len(split), top_value / len(split)))
        gain = gain * jnp.repeat(heights, dims[position] // shards_of).reshape([-1 if axis == position else 1 for axis in range(len(dims))])
    return gain


def routed_block(key, own, number, rows, count, top, bound, lean):
    order = jax.random.permutation(key, count)
    crowded, common = load_shares(count, rows * top, bound, lean, True), load_shares(count, rows * top, bound, lean, False)
    places = jnp.arange(count)

    def named(tallies, offset_by):
        used = int((tallies > 0).sum())
        fixed = max(1, used // 4)
        moved = fixed + (places - fixed + offset_by * (used - fixed)) % max(1, count - fixed)
        return jnp.zeros((count,), jnp.int32).at[order[jnp.where(places < fixed, places, moved)]].set(jnp.asarray(tallies, jnp.int32))

    tallies = jnp.where(number % 4 == 0, named(crowded, number // 4), named(common, number - number // 4 - 1))
    mixed = jax.random.permutation(jax.random.fold_in(own, 3), count)
    source_of, sink = mixed[0:count // 2 * 2:2], mixed[1:count // 2 * 2:2]
    margin = jnp.minimum(tallies[source_of] - 1, bound - tallies[sink]) // 2
    margin = jnp.where((source_of == order[0]) | (sink == order[0]) | (tallies[sink] == 0), 0, jnp.maximum(margin, 0))
    moved = jax.random.randint(jax.random.fold_in(own, 4), (count // 2,), 0, 1 << 20) % (margin + 1)
    tallies = tallies.at[source_of].add(-moved).at[sink].add(moved)
    labels = jnp.searchsorted(jnp.cumsum(tallies), jnp.arange(rows * top), side="right").astype(jnp.int32)
    table = labels.reshape(top, rows).T
    table = table[jax.random.permutation(jax.random.fold_in(own, 1), rows)]
    offset_by = jax.random.randint(jax.random.fold_in(own, 2), (rows, 1), 0, top)
    return jnp.take_along_axis(table, (jnp.arange(top)[None, :] + offset_by) % top, axis=1)


def load_shares(number_of, total, bound, skew, full):
    weights = [(1 << 20) // math.isqrt(rank ** skew) + 1 for rank in range(1, number_of + 1)]
    largest = bound if full else min(bound, max(-(-total // number_of), total * weights[0] // sum(weights)))
    least = 1 if total - largest >= number_of - 1 else 0
    holding, surplus = [largest] + [least] * (number_of - 1), total - largest - least * (number_of - 1)
    while surplus > 0:
        candidates = [i for i in range(1, number_of) if holding[i] < largest] or [i for i in range(1, number_of) if holding[i] < bound]
        whole, remaining = sum([weights[i] for i in candidates]), surplus
        for i in candidates:
            extra = min(bound - holding[i], max(1, remaining * weights[i] // whole), surplus)
            holding[i] = holding[i] + extra
            surplus = surplus - extra
    return np.array(holding)


def scatter_about(rng, dims, width, bound, cuts=(), held_as=jnp.bfloat16):
    factor_of = level_of(rng, dims, cuts, -0.22, 0.18) if cuts else 1.0
    result = jax.random.normal(rng, dims, jnp.float32) * width * factor_of
    return jnp.minimum(jnp.maximum(result, -bound), bound).astype(held_as)


def setup_inputs(seed: int = 0) -> dict:
    key_of = jax.random.split(jax.random.key(seed), 16)
    residual_in = draw_residual_in(jax.random.fold_in(key_of[15], 71), 0)
    queries = draw_queries(jax.random.fold_in(key_of[15], 71), 0)
    fresh_token_keys = scatter_about(key_of[2], (REQUEST_TOTAL, KEY_VALUE_HEADS * HEAD_SIZE), 1.0, 6.0, ((0, 8), (1, 4)))
    fresh_token_values = scatter_about(key_of[3], (REQUEST_TOTAL, KEY_VALUE_HEADS * HEAD_SIZE), 1.0, 6.0, ((0, 8), (1, 4)))
    cached_key_slots = scatter_about(key_of[4], (REQUEST_TOTAL, LONGEST_LENGTH, KEY_VALUE_HEADS * HEAD_SIZE), 1.0, 6.0, ((0, 8), (2, 4)))
    cached_value_slots = scatter_about(key_of[5], (REQUEST_TOTAL, LONGEST_LENGTH, KEY_VALUE_HEADS * HEAD_SIZE), 1.0, 6.0, ((0, 8), (2, 4)))
    lengths = draw_lengths(jax.random.fold_in(key_of[15], 71), 0)
    slot_order = draw_slot_order(jax.random.fold_in(key_of[15], 71), 0)
    out_proj = scatter_about(key_of[8], (QUERY_HEADS * HEAD_SIZE, D), HEAD_SIZE ** -0.5, 0.5, ((0, 4),))
    norm_gain = jnp.clip(1.0 + 0.1 * jax.random.normal(key_of[9], (D,), jnp.float32), 0.5, 1.5).astype(jnp.bfloat16)
    expert_ids_keys = jax.random.split(jax.random.fold_in(key_of[10], 1), REQUEST_TOTAL // REQUEST_TOTAL)
    expert_ids_turns = jax.random.permutation(jax.random.fold_in(key_of[10], 3), REQUEST_TOTAL // REQUEST_TOTAL)
    expert_ids = jax.vmap(lambda own, number: routed_block(jax.random.fold_in(key_of[10], 2), own, number, REQUEST_TOTAL, NE, TOPK, CAPE, 1))(expert_ids_keys, expert_ids_turns).reshape((REQUEST_TOTAL, TOPK))
    gate_values = jnp.clip(jax.random.uniform(key_of[11], (REQUEST_TOTAL, TOPK), jnp.float32, 0.1, 0.5), 0.1, 0.5)
    gate_proj = scatter_about(key_of[12], (NE, D, FE), D ** -0.5, 0.125, ((0, 8), (2, 4)))
    up_proj = scatter_about(key_of[13], (NE, D, FE), D ** -0.5, 0.125, ((0, 8), (2, 4)))
    down_proj = scatter_about(key_of[14], (NE, FE, D), FE ** -0.5, 0.15625, ((0, 8), (1, 4)))
    return dict(residual_in=residual_in, queries=queries, fresh_token_keys=fresh_token_keys, fresh_token_values=fresh_token_values, cached_key_slots=cached_key_slots, cached_value_slots=cached_value_slots, lengths=lengths, slot_order=slot_order, out_proj=out_proj, norm_gain=norm_gain, expert_ids=expert_ids, gate_values=gate_values, gate_proj=gate_proj, up_proj=up_proj, down_proj=down_proj)


def attend_slot(rows_per_head, request_key, request_value, gathered_keys, gathered_values, length):
    rows_per_head = rows_per_head.reshape(KEY_VALUE_HEADS, QUERY_HEADS // KEY_VALUE_HEADS, HEAD_SIZE).astype(jnp.float32)
    gathered_keys = gathered_keys.reshape(LONGEST_LENGTH, KEY_VALUE_HEADS, HEAD_SIZE).astype(jnp.float32)
    gathered_values = gathered_values.reshape(LONGEST_LENGTH, KEY_VALUE_HEADS, HEAD_SIZE).astype(jnp.float32)
    self_key_row = request_key.reshape(KEY_VALUE_HEADS, HEAD_SIZE).astype(jnp.float32)
    self_value_row = request_value.reshape(KEY_VALUE_HEADS, HEAD_SIZE).astype(jnp.float32)
    inv_root = 1.0 / math.sqrt(HEAD_SIZE)
    scores = jnp.einsum('gqd,lgd->gql', rows_per_head, gathered_keys) * inv_root
    positions = jnp.arange(LONGEST_LENGTH)
    scores = jnp.where((positions < length)[None, None, :], scores, -1e+30)
    own_score = jnp.einsum('gqd,gd->gq', rows_per_head, self_key_row) * inv_root
    highest = jnp.maximum(lax.optimization_barrier(jnp.max(scores, axis=2)), own_score)
    weights = jnp.exp(scores - highest[:, :, None])
    own_weight = jnp.exp(own_score - highest)
    totals = lax.optimization_barrier(jnp.sum(weights, axis=2)) + own_weight
    weights_low = lax.optimization_barrier(weights.astype(jnp.bfloat16)).astype(jnp.float32)
    own_low = lax.optimization_barrier(own_weight.astype(jnp.bfloat16)).astype(jnp.float32)
    numerator = jnp.einsum('gql,lgd->gqd', weights_low, gathered_values) + own_low[:, :, None] * self_value_row[:, None, :]
    return (numerator / totals[:, :, None]).astype(jnp.bfloat16).reshape(QUERY_HEADS * HEAD_SIZE)

def attend_pack(packed):
    return attend_slot(*packed)

def reference(residual_in, queries, fresh_token_keys, fresh_token_values, cached_key_slots, cached_value_slots, lengths, slot_order, out_proj, norm_gain, expert_ids, gate_values, gate_proj, up_proj, down_proj):
    slot_len = lengths[slot_order]
    attended = lax.map(attend_pack, (queries[slot_order], fresh_token_keys[slot_order], fresh_token_values[slot_order], cached_key_slots, cached_value_slots, slot_len))
    projected = jnp.dot(attended, out_proj, preferred_element_type=jnp.float32)
    by_request = jnp.zeros((REQUEST_TOTAL, D), jnp.float32).at[slot_order].set(projected)
    hidden = residual_in.astype(jnp.float32) + by_request
    mean_sq = lax.optimization_barrier(jnp.sum(hidden * hidden, axis=1)) / D
    normed = (hidden * lax.rsqrt(mean_sq + 1e-06)[:, None] * norm_gain.astype(jnp.float32)).astype(jnp.bfloat16)
    flat_ids = expert_ids.reshape(-1)
    flat_gates = gate_values.reshape(-1)

    def expert_step(mixture, expert):
        picked = jnp.argsort((flat_ids != expert).astype(jnp.int32), stable=True)[:CAPE].astype(jnp.int32)
        chosen = flat_ids[picked] == expert
        token_idx = (picked // TOPK).astype(jnp.int32)
        row_block = normed[token_idx]
        gate_h = jnp.dot(row_block, gate_proj[expert], preferred_element_type=jnp.float32)
        up_h = jnp.dot(row_block, up_proj[expert], preferred_element_type=jnp.float32)
        inner_act = (jax.nn.silu(gate_h) * up_h).astype(jnp.bfloat16)
        outputs = jnp.dot(inner_act, down_proj[expert], preferred_element_type=jnp.float32)
        token_gate = jnp.where(chosen, flat_gates[picked], jnp.zeros_like(flat_gates[picked]))
        return (mixture.at[token_idx].add(outputs * token_gate[:, None]), None)
    mixture, _ = lax.scan(expert_step, jnp.zeros((REQUEST_TOTAL, D), jnp.float32), jnp.arange(NE, dtype=jnp.int32))
    return (hidden + mixture).astype(jnp.bfloat16)
```

```python
import functools
import math

import jax
import jax.numpy as jnp
from jax import lax
from jax.experimental import pallas as pl
from jax.experimental.pallas import tpu as pltpu
from jax.sharding import PartitionSpec as P

MESH = pl.DeviceIdType.MESH
F32 = jnp.float32
BF16 = jnp.bfloat16

PART_TYPE = F32
LAST_TYPE = F32


def layer_kernel(
    n_req,
    n_kv,
    len_ref,
    order_ref,
    ids_ref,
    gates_ref,
    gain_ref,
    res_hbm,
    q_hbm,
    k_hbm,
    v_hbm,
    keys_hbm,
    values_hbm,
    wo_hbm,
    wg_hbm,
    wu_hbm,
    wd_hbm,
    out_ref,
    rows,
    gains,
    keys,
    values,
    wo,
    wg,
    wu,
    wd,
    qmat,
    att,
    mine,
    part,
    normed,
    tokens,
    ysend,
    yrecv,
    zsend,
    zrecv,
    in_sem,
    w_sem,
    kv_send,
    kv_recv,
    req_send,
    req_recv,
):
    r = lax.axis_index("req")
    f = lax.axis_index("kv")
    per_dev, width = mine.shape
    q_width = q_hbm.shape[1]
    hd = k_hbm.shape[1]
    chunk = res_hbm.shape[1]
    heads = q_width // hd
    longest = keys.shape[1]
    total = n_req * per_dev

    places = (
        (q_hbm, 0, q_width),
        (k_hbm, q_width, hd),
        (v_hbm, q_width + hd, hd),
        (res_hbm, q_width + 2 * hd, chunk),
    )
    small = [
        pltpu.make_async_copy(src, rows.at[0, :, pl.ds(at, size)], in_sem.at[i])
        for i, (src, at, size) in enumerate(places)
    ]
    for c in small:
        c.start()
    loads = []
    for i in range(per_dev):
        loads.append(pltpu.make_async_copy(keys_hbm.at[i], keys.at[i], w_sem.at[2 * i]))
        loads.append(pltpu.make_async_copy(values_hbm.at[i], values.at[i], w_sem.at[2 * i + 1]))
    base = 2 * per_dev
    load_wo = pltpu.make_async_copy(wo_hbm, wo, w_sem.at[base])
    load_wg = pltpu.make_async_copy(wg_hbm.at[0], wg, w_sem.at[base + 1])
    load_wu = pltpu.make_async_copy(wu_hbm.at[0], wu, w_sem.at[base + 2])
    load_wd = pltpu.make_async_copy(wd_hbm.at[0], wd, w_sem.at[base + 3])
    for c in (*loads, load_wo, load_wg, load_wu, load_wd):
        c.start()

    def req_peer(d):
        return lax.rem(r + d, n_req)

    def kv_peer(k):
        return lax.rem(f + k, n_kv)

    barrier = pltpu.get_barrier_semaphore()
    for d in range(1, n_req):
        pl.semaphore_signal(barrier, inc=1, device_id=(req_peer(d), f), device_id_type=MESH)
    for k in range(1, n_kv):
        pl.semaphore_signal(barrier, inc=1, device_id=(r, kv_peer(k)), device_id_type=MESH)

    own_columns = pl.ds(pl.multiple_of(f * chunk, chunk), chunk)
    gains[:, own_columns] = gain_ref[...].astype(F32)
    qmat[...] = jnp.zeros_like(qmat)
    att[...] = jnp.zeros_like(att)

    for c in small:
        c.wait()
    pl.semaphore_wait(barrier, n_req + n_kv - 2)

    def to_req(stage, d, src, dst):
        return pltpu.make_async_remote_copy(
            src_ref=src,
            dst_ref=dst,
            send_sem=req_send.at[stage, d],
            recv_sem=req_recv.at[stage, d],
            device_id=(req_peer(d), f),
            device_id_type=MESH,
        )

    def to_kv(stage, k, src, dst):
        return pltpu.make_async_remote_copy(
            src_ref=src,
            dst_ref=dst,
            send_sem=kv_send.at[stage, k],
            recv_sem=kv_recv.at[stage, k],
            device_id=(r, kv_peer(k)),
            device_id_type=MESH,
        )

    first = [to_req(0, d, rows.at[0], rows.at[d]) for d in range(1, n_req)]
    for c in first:
        c.start()
    own_gain = gains.at[:, own_columns]
    gain_out = [to_kv(0, k, own_gain, own_gain) for k in range(1, n_kv)]
    for c in gain_out:
        c.start()
    for c in first:
        c.wait_recv()

    inv_root = 1.0 / math.sqrt(hd)
    served = [order_ref[r * per_dev + i] for i in range(per_dev)]
    positions = lax.broadcasted_iota(jnp.int32, (1, longest), 1)
    residual = []
    for i in range(per_dev):
        t = served[i]
        src = t // per_dev
        pair = rows[lax.rem(r - src + n_req, n_req)].astype(F32)
        which = lax.broadcasted_iota(jnp.int32, pair.shape, 0) == t - src * per_dev
        row = jnp.sum(jnp.where(which, pair, 0.0), axis=0, keepdims=True)
        residual.append(row[:, q_width + 2 * hd :])
        k_row = row[:, q_width : q_width + hd]
        v_row = row[:, q_width + hd : q_width + 2 * hd]
        for h in range(heads):
            qmat[i, h : h + 1, :] = row[:, h * hd : (h + 1) * hd]
        q = qmat[i]
        loads[2 * i].wait()
        scores = (
            lax.dot_general(
                q.astype(BF16), keys[i], (((1,), (1,)), ((), ())), preferred_element_type=F32
            )
            * inv_root
        )
        scores = jnp.where(positions < len_ref[t], scores, -1e30)
        own = jnp.sum(q * k_row, axis=1, keepdims=True) * inv_root
        highest = jnp.maximum(jnp.max(scores, axis=1, keepdims=True), own)
        weights = jnp.exp(scores - highest)
        own_weight = jnp.exp(own - highest)
        totals = jnp.sum(weights, axis=1, keepdims=True) + own_weight
        loads[2 * i + 1].wait()
        numerator = jnp.dot(weights.astype(BF16), values[i], preferred_element_type=F32)
        numerator = numerator + own_weight.astype(BF16).astype(F32) * v_row
        attended = numerator / totals
        for h in range(heads):
            att[i : i + 1, h * hd : (h + 1) * hd] = attended[h : h + 1, :]

    load_wo.wait()
    projected = jnp.dot(att[...].astype(BF16), wo[...], preferred_element_type=F32)
    mine[...] = projected[:per_dev]
    mine[:, own_columns] += jnp.concatenate(residual, axis=0)
    part[0] = mine[...].astype(part.dtype)
    second = [to_kv(1, k, part.at[0], part.at[k]) for k in range(1, n_kv)]
    for c in second:
        c.start()
    for c in gain_out:
        c.wait_recv()
    for c in second:
        c.wait_recv()
    hidden = mine[...]
    for k in range(1, n_kv):
        hidden = hidden + part[k].astype(F32)
    mine[...] = hidden
    squares = jnp.sum(hidden * hidden, axis=1, keepdims=True)
    normed[0] = (hidden * lax.rsqrt(squares / width + 1e-06) * gains[...]).astype(BF16)

    third = [to_req(1, d, normed.at[0], normed.at[d]) for d in range(1, n_req)]
    for c in third:
        c.start()

    gate_row = jnp.sum(jnp.where(ids_ref[...] == r, gates_ref[...], 0.0), axis=0, keepdims=True)
    token_of = lax.broadcasted_iota(jnp.int32, (total, total), 0)
    other_of = lax.broadcasted_iota(jnp.int32, (total, total), 1)
    gate = jnp.sum(jnp.where(token_of == other_of, gate_row, 0.0), axis=1, keepdims=True)
    slot_row = jnp.zeros((1, total), jnp.int32)
    slot_at = lax.broadcasted_iota(jnp.int32, (1, total), 1)
    for d in range(n_req):
        src = lax.rem(r - d + n_req, n_req)
        for i in range(per_dev):
            slot_row = jnp.where(
                slot_at == d * per_dev + i, order_ref[src * per_dev + i], slot_row
            )
    to_token = jnp.where(token_of == slot_row, 1.0, 0.0).astype(BF16)
    hidden_part = mine[:, own_columns]
    token_at = lax.broadcasted_iota(jnp.int32, (total, 1), 0)
    placed = jnp.zeros((total, chunk), F32)
    for i in range(per_dev):
        placed = placed + jnp.where(token_at == served[i], hidden_part[i : i + 1, :], 0.0)
    tokens[0:per_dev, :] = normed[0].astype(F32)
    load_wg.wait()
    load_wu.wait()
    load_wd.wait()

    for d, c in enumerate(third, 1):
        c.wait_recv()
        tokens[d * per_dev : (d + 1) * per_dev, :] = normed[d].astype(F32)
    x = tokens[...].astype(BF16)
    gate_h = jnp.dot(x, wg[...], preferred_element_type=F32)
    up_h = jnp.dot(x, wu[...], preferred_element_type=F32)
    inner = (gate_h / (1.0 + jnp.exp(-gate_h)) * up_h).astype(BF16)
    inner = jnp.dot(to_token, inner, preferred_element_type=F32).astype(BF16)

    fourth = []
    for k in range(1, n_kv):
        columns = pl.ds(pl.multiple_of(kv_peer(k) * chunk, chunk), chunk)
        y = jnp.dot(inner, wd[:, columns], preferred_element_type=F32) * gate
        ysend[k - 1] = y.astype(BF16)
        c = to_kv(2, k, ysend.at[k - 1], yrecv.at[k - 1])
        c.start()
        fourth.append(c)
    y = jnp.dot(inner, wd[:, own_columns], preferred_element_type=F32) * gate + placed
    for k, c in enumerate(fourth):
        c.wait_recv()
        y = y + yrecv[k].astype(F32)
    for p in range(n_req):
        zsend[p] = y[p * per_dev : (p + 1) * per_dev, :].astype(zsend.dtype)
    fifth = [to_req(2, d, zsend.at[req_peer(d)], zrecv.at[d - 1]) for d in range(1, n_req)]
    for c in fifth:
        c.start()
    z = zsend[r].astype(F32)
    for d, c in enumerate(fifth):
        c.wait_recv()
        z = z + zrecv[d].astype(F32)
    out_ref[...] = z.astype(out_ref.dtype)
    for c in (*first, *gain_out, *second, *third, *fourth, *fifth):
        c.wait_send()


def per_device(
    residual_in,
    queries,
    fresh_token_keys,
    fresh_token_values,
    cached_key_slots,
    cached_value_slots,
    lengths,
    slot_order,
    out_proj,
    norm_gain,
    expert_ids,
    gate_values,
    gate_proj,
    up_proj,
    down_proj,
):
    n_req = lax.axis_size("req")
    n_kv = lax.axis_size("kv")
    per_dev, chunk = residual_in.shape
    q_width = queries.shape[1]
    hd = fresh_token_keys.shape[1]
    width = out_proj.shape[1]
    total = lengths.shape[0]
    row_width = q_width + 2 * hd + chunk
    heads_up = -(-(q_width // hd) // 8) * 8
    vmem = pl.BlockSpec(memory_space=pltpu.VMEM)
    smem = pl.BlockSpec(memory_space=pltpu.SMEM)
    hbm = pl.BlockSpec(memory_space=pl.ANY)
    return pl.pallas_call(
        functools.partial(layer_kernel, n_req, n_kv),
        out_shape=jax.ShapeDtypeStruct((per_dev, chunk), BF16),
        in_specs=[smem, smem, vmem, vmem, vmem] + [hbm] * 10,
        out_specs=vmem,
        scratch_shapes=[
            pltpu.VMEM((n_req, per_dev, row_width), BF16),
            pltpu.VMEM((1, width), F32),
            pltpu.VMEM(cached_key_slots.shape, BF16),
            pltpu.VMEM(cached_value_slots.shape, BF16),
            pltpu.VMEM(out_proj.shape, BF16),
            pltpu.VMEM(gate_proj.shape[1:], BF16),
            pltpu.VMEM(up_proj.shape[1:], BF16),
            pltpu.VMEM(down_proj.shape[1:], BF16),
            pltpu.VMEM((per_dev, heads_up, hd), F32),
            pltpu.VMEM((8, q_width), F32),
            pltpu.VMEM((per_dev, width), F32),
            pltpu.VMEM((n_kv, per_dev, width), PART_TYPE),
            pltpu.VMEM((n_req, per_dev, width), BF16),
            pltpu.VMEM((total, width), F32),
            pltpu.VMEM((n_kv - 1, total, chunk), BF16),
            pltpu.VMEM((n_kv - 1, total, chunk), BF16),
            pltpu.VMEM((n_req, per_dev, chunk), LAST_TYPE),
            pltpu.VMEM((n_req - 1, per_dev, chunk), LAST_TYPE),
            pltpu.SemaphoreType.DMA((4,)),
            pltpu.SemaphoreType.DMA((2 * per_dev + 4,)),
            pltpu.SemaphoreType.DMA((3, n_kv)),
            pltpu.SemaphoreType.DMA((3, n_kv)),
            pltpu.SemaphoreType.DMA((3, n_req)),
            pltpu.SemaphoreType.DMA((3, n_req)),
        ],
        compiler_params=pltpu.CompilerParams(
            collective_id=0, has_side_effects=True, vmem_limit_bytes=56 * 1024 * 1024
        ),
        cost_estimate=pl.CostEstimate(
            flops=400_000_000, bytes_accessed=14_000_000, transcendentals=100_000
        ),
    )(
        lengths,
        slot_order,
        expert_ids.T,
        gate_values.T,
        norm_gain.reshape(1, -1),
        residual_in,
        queries,
        fresh_token_keys,
        fresh_token_values,
        cached_key_slots,
        cached_value_slots,
        out_proj,
        gate_proj,
        up_proj,
        down_proj,
    )


def solution(mesh):
    in_specs = (
        P("req", "kv"),
        P("req", "kv"),
        P("req", "kv"),
        P("req", "kv"),
        P("req", None, "kv"),
        P("req", None, "kv"),
        P(),
        P(),
        P("kv", None),
        P("kv"),
        P(),
        P(),
        P("req", None, "kv"),
        P("req", None, "kv"),
        P("req", "kv", None),
    )
    return jax.shard_map(
        per_device, mesh=mesh, in_specs=in_specs, out_specs=P("req", "kv"), check_vma=False
    )
```

```python
import functools
import math

import jax
import jax.numpy as jnp
from jax import lax
from jax.experimental import pallas as pl
from jax.experimental.pallas import tpu as pltpu
from jax.sharding import PartitionSpec as P

MESH = pl.DeviceIdType.MESH
F32 = jnp.float32
BF16 = jnp.bfloat16

PART_TYPE = BF16
LAST_TYPE = BF16


def layer_kernel(
    n_req,
    n_kv,
    len_hbm,
    order_hbm,
    ids_hbm,
    gates_hbm,
    gain_hbm,
    res_hbm,
    q_hbm,
    k_hbm,
    v_hbm,
    keys_hbm,
    values_hbm,
    wo_hbm,
    wg_hbm,
    wu_hbm,
    wd_hbm,
    out_ref,
    rows,
    gains,
    keys,
    values,
    wo,
    wg,
    wu,
    wd,
    qmat,
    att,
    mine,
    part,
    normed,
    tokens,
    zsend,
    zrecv,
    in_sem,
    w_sem,
    kv_send,
    kv_recv,
    req_send,
    req_recv,
    z_sems,
    len_ref,
    order_ref,
    ids_ref,
    gates_ref,
    gain_ref,
    aux_sem,
):
    r = lax.axis_index("req")
    f = lax.axis_index("kv")
    per_dev, width = mine.shape
    q_width = q_hbm.shape[1]
    hd = k_hbm.shape[1]
    chunk = res_hbm.shape[1]
    heads = q_width // hd
    longest = keys.shape[1]
    total = n_req * per_dev

    def req_peer(d):
        return lax.rem(r + d, n_req)

    def kv_peer(k):
        return lax.rem(f + k, n_kv)

    barrier = pltpu.get_barrier_semaphore()
    for d in range(n_req - 1, -1, -1):
        for k in range(n_kv):
            if d or k:
                pl.semaphore_signal(
                    barrier, inc=1, device_id=(req_peer(d), kv_peer(k)), device_id_type=MESH
                )

    places = (
        (q_hbm, 0, q_width),
        (k_hbm, q_width, hd),
        (v_hbm, q_width + hd, hd),
        (res_hbm, q_width + 2 * hd, chunk),
    )
    small = [
        pltpu.make_async_copy(src, rows.at[0, :, pl.ds(at, size)], in_sem.at[i])
        for i, (src, at, size) in enumerate(places)
    ]
    for c in small:
        c.start()
    gain_in = pltpu.make_async_copy(gain_hbm, gain_ref, aux_sem.at[0])
    aux = [
        pltpu.make_async_copy(src, dst, aux_sem.at[i])
        for i, (src, dst) in enumerate(
            (
                (len_hbm, len_ref),
                (order_hbm, order_ref),
                (ids_hbm, ids_ref),
                (gates_hbm, gates_ref),
            ),
            1,
        )
    ]
    for c in (gain_in, *aux):
        c.start()
    loads = []
    for i in range(per_dev):
        loads.append(pltpu.make_async_copy(keys_hbm.at[i], keys.at[i], w_sem.at[2 * i]))
        loads.append(pltpu.make_async_copy(values_hbm.at[i], values.at[i], w_sem.at[2 * i + 1]))
    base = 2 * per_dev
    load_wo = pltpu.make_async_copy(wo_hbm, wo, w_sem.at[base])
    load_wg = pltpu.make_async_copy(wg_hbm.at[0], wg, w_sem.at[base + 1])
    load_wu = pltpu.make_async_copy(wu_hbm.at[0], wu, w_sem.at[base + 2])
    load_wd = pltpu.make_async_copy(wd_hbm.at[0], wd, w_sem.at[base + 3])
    for c in loads:
        c.start()

    own_columns = pl.ds(pl.multiple_of(f * chunk, chunk), chunk)
    gain_in.wait()
    gains[:, own_columns] = gain_ref[...].astype(F32).reshape(1, -1)
    qmat[...] = jnp.zeros_like(qmat)
    att[...] = jnp.zeros_like(att)

    for c in small:
        c.wait()
    pl.semaphore_wait(barrier, n_req * n_kv - 1)

    def to_req(stage, d, src, dst):
        return pltpu.make_async_remote_copy(
            src_ref=src,
            dst_ref=dst,
            send_sem=req_send.at[stage, d],
            recv_sem=req_recv.at[stage, d],
            device_id=(req_peer(d), f),
            device_id_type=MESH,
        )

    def to_kv(stage, k, src, dst):
        return pltpu.make_async_remote_copy(
            src_ref=src,
            dst_ref=dst,
            send_sem=kv_send.at[stage, k],
            recv_sem=kv_recv.at[stage, k],
            device_id=(r, kv_peer(k)),
            device_id_type=MESH,
        )

    first = [to_req(0, d, rows.at[0], rows.at[d]) for d in range(1, n_req)]
    for c in first:
        c.start()
    own_gain = gains.at[:, own_columns]
    for c in (load_wo, load_wg, load_wu, load_wd):
        c.start()
    gain_out = [to_kv(0, k, own_gain, own_gain) for k in range(1, n_kv)]
    for c in gain_out:
        c.start()
    for c in (*aux, *loads, load_wo):
        c.wait()
    for c in first:
        c.wait_recv()

    inv_root = 1.0 / math.sqrt(hd)
    served = [order_ref[r * per_dev + i] for i in range(per_dev)]
    positions = lax.broadcasted_iota(jnp.int32, (1, longest), 1)
    residual = []
    for i in range(per_dev):
        t = served[i]
        src = t // per_dev
        pair = rows[lax.rem(r - src + n_req, n_req)].astype(F32)
        which = lax.broadcasted_iota(jnp.int32, pair.shape, 0) == t - src * per_dev
        row = jnp.sum(jnp.where(which, pair, 0.0), axis=0, keepdims=True)
        residual.append(row[:, q_width + 2 * hd :])
        k_row = row[:, q_width : q_width + hd]
        v_row = row[:, q_width + hd : q_width + 2 * hd]
        for h in range(heads):
            qmat[i, h : h + 1, :] = row[:, h * hd : (h + 1) * hd]
        q = qmat[i]
        scores = (
            lax.dot_general(
                q.astype(BF16), keys[i], (((1,), (1,)), ((), ())), preferred_element_type=F32
            )
            * inv_root
        )
        scores = jnp.where(positions < len_ref[t], scores, -1e30)
        own = jnp.sum(q * k_row, axis=1, keepdims=True) * inv_root
        highest = jnp.maximum(jnp.max(scores, axis=1, keepdims=True), own)
        weights = jnp.exp(scores - highest)
        own_weight = jnp.exp(own - highest)
        totals = jnp.sum(weights, axis=1, keepdims=True) + own_weight
        numerator = jnp.dot(weights.astype(BF16), values[i], preferred_element_type=F32)
        numerator = numerator + own_weight.astype(BF16).astype(F32) * v_row
        attended = numerator / totals
        for h in range(heads):
            att[i : i + 1, h * hd : (h + 1) * hd] = attended[h : h + 1, :]

    projected = jnp.dot(att[...].astype(BF16), wo[...], preferred_element_type=F32)
    mine[...] = projected[:per_dev]
    mine[:, own_columns] += jnp.concatenate(residual, axis=0)
    part[0] = mine[...].astype(part.dtype)
    second = [to_kv(1, k, part.at[0], part.at[k]) for k in range(1, n_kv)]
    for c in second:
        c.start()
    for c in gain_out:
        c.wait_recv()
    for c in second:
        c.wait_recv()
    hidden = mine[...]
    for k in range(1, n_kv):
        hidden = hidden + part[k].astype(F32)
    mine[...] = hidden
    squares = jnp.sum(hidden * hidden, axis=1, keepdims=True)
    normed[0] = (hidden * lax.rsqrt(squares / width + 1e-06) * gains[...]).astype(BF16)

    third = [to_req(1, d, normed.at[0], normed.at[d]) for d in range(1, n_req)]
    for c in third:
        c.start()

    gate_row = jnp.sum(jnp.where(ids_ref[...] == r, gates_ref[...], 0.0), axis=0, keepdims=True)
    token_of = lax.broadcasted_iota(jnp.int32, (total, total), 0)
    other_of = lax.broadcasted_iota(jnp.int32, (total, total), 1)
    gate = jnp.sum(jnp.where(token_of == other_of, gate_row, 0.0), axis=1, keepdims=True)
    slot_row = jnp.zeros((1, total), jnp.int32)
    slot_at = lax.broadcasted_iota(jnp.int32, (1, total), 1)
    for d in range(n_req):
        src = lax.rem(r - d + n_req, n_req)
        for i in range(per_dev):
            slot_row = jnp.where(
                slot_at == d * per_dev + i, order_ref[src * per_dev + i], slot_row
            )
    to_token = jnp.where(token_of == slot_row, 1.0, 0.0).astype(BF16)
    hidden_part = mine[:, own_columns]
    token_at = lax.broadcasted_iota(jnp.int32, (total, 1), 0)
    placed = jnp.zeros((total, chunk), F32)
    for i in range(per_dev):
        placed = placed + jnp.where(token_at == served[i], hidden_part[i : i + 1, :], 0.0)
    tokens[0:per_dev, :] = normed[0].astype(F32)
    load_wg.wait()
    load_wu.wait()
    load_wd.wait()

    for d, c in enumerate(third, 1):
        c.wait_recv()
        tokens[d * per_dev : (d + 1) * per_dev, :] = normed[d].astype(F32)
    x = tokens[...].astype(BF16)
    gate_h = jnp.dot(x, wg[...], preferred_element_type=F32)
    up_h = jnp.dot(x, wu[...], preferred_element_type=F32)
    inner = (gate_h / (1.0 + jnp.exp(-gate_h)) * up_h).astype(BF16)
    inner = jnp.dot(to_token, inner, preferred_element_type=F32).astype(BF16)

    fourth = []
    for k in (*range(1, n_kv), 0):
        columns = pl.ds(pl.multiple_of(kv_peer(k) * chunk, chunk), chunk)
        y = jnp.dot(inner, wd[:, columns], preferred_element_type=F32) * gate
        if k == 0:
            y = y + placed
        y = y.astype(zsend.dtype)
        for p in range(n_req):
            zsend[k, p] = y[p * per_dev : (p + 1) * per_dev, :]
        for d in range(n_req):
            if k == 0 and d == 0:
                continue
            c = pltpu.make_async_remote_copy(
                src_ref=zsend.at[k, req_peer(d)],
                dst_ref=zrecv.at[k, d],
                send_sem=z_sems.at[0, k * n_req + d],
                recv_sem=z_sems.at[1, k * n_req + d],
                device_id=(req_peer(d), kv_peer(k)),
                device_id_type=MESH,
            )
            c.start()
            fourth.append((k, d, c))
    z = zsend[0, r].astype(F32)
    for k, d, c in fourth:
        c.wait_recv()
        z = z + zrecv[k, d].astype(F32)
    out_ref[...] = z.astype(out_ref.dtype)
    for c in (*first, *gain_out, *second, *third):
        c.wait_send()
    for _, _, c in fourth:
        c.wait_send()


def per_device(
    residual_in,
    queries,
    fresh_token_keys,
    fresh_token_values,
    cached_key_slots,
    cached_value_slots,
    lengths,
    slot_order,
    out_proj,
    norm_gain,
    expert_ids,
    gate_values,
    gate_proj,
    up_proj,
    down_proj,
):
    n_req = lax.axis_size("req")
    n_kv = lax.axis_size("kv")
    per_dev, chunk = residual_in.shape
    q_width = queries.shape[1]
    hd = fresh_token_keys.shape[1]
    width = out_proj.shape[1]
    total = lengths.shape[0]
    row_width = q_width + 2 * hd + chunk
    heads_up = -(-(q_width // hd) // 8) * 8
    vmem = pl.BlockSpec(memory_space=pltpu.VMEM)
    hbm = pl.BlockSpec(memory_space=pl.ANY)
    return pl.pallas_call(
        functools.partial(layer_kernel, n_req, n_kv),
        out_shape=jax.ShapeDtypeStruct((per_dev, chunk), BF16),
        in_specs=[hbm] * 15,
        out_specs=vmem,
        scratch_shapes=[
            pltpu.VMEM((n_req, per_dev, row_width), BF16),
            pltpu.VMEM((1, width), F32),
            pltpu.VMEM(cached_key_slots.shape, BF16),
            pltpu.VMEM(cached_value_slots.shape, BF16),
            pltpu.VMEM(out_proj.shape, BF16),
            pltpu.VMEM(gate_proj.shape[1:], BF16),
            pltpu.VMEM(up_proj.shape[1:], BF16),
            pltpu.VMEM(down_proj.shape[1:], BF16),
            pltpu.VMEM((per_dev, heads_up, hd), F32),
            pltpu.VMEM((8, q_width), F32),
            pltpu.VMEM((per_dev, width), F32),
            pltpu.VMEM((n_kv, per_dev, width), PART_TYPE),
            pltpu.VMEM((n_req, per_dev, width), BF16),
            pltpu.VMEM((total, width), F32),
            pltpu.VMEM((n_kv, n_req, per_dev, chunk), LAST_TYPE),
            pltpu.VMEM((n_kv, n_req, per_dev, chunk), LAST_TYPE),
            pltpu.SemaphoreType.DMA((4,)),
            pltpu.SemaphoreType.DMA((2 * per_dev + 4,)),
            pltpu.SemaphoreType.DMA((2, n_kv)),
            pltpu.SemaphoreType.DMA((2, n_kv)),
            pltpu.SemaphoreType.DMA((2, n_req)),
            pltpu.SemaphoreType.DMA((2, n_req)),
            pltpu.SemaphoreType.DMA((2, n_kv * n_req)),
            pltpu.SMEM(lengths.shape, jnp.int32),
            pltpu.SMEM(slot_order.shape, jnp.int32),
            pltpu.VMEM(expert_ids.shape[::-1], jnp.int32),
            pltpu.VMEM(gate_values.shape[::-1], F32),
            pltpu.VMEM(norm_gain.shape, BF16),
            pltpu.SemaphoreType.DMA((5,)),
        ],
        compiler_params=pltpu.CompilerParams(
            collective_id=0, has_side_effects=True, vmem_limit_bytes=56 * 1024 * 1024
        ),
        cost_estimate=pl.CostEstimate(
            flops=400_000_000, bytes_accessed=14_000_000, transcendentals=100_000
        ),
    )(
        lengths,
        slot_order,
        expert_ids.T,
        gate_values.T,
        norm_gain,
        residual_in,
        queries,
        fresh_token_keys,
        fresh_token_values,
        cached_key_slots,
        cached_value_slots,
        out_proj,
        gate_proj,
        up_proj,
        down_proj,
    )


def solution(mesh):
    in_specs = (
        P("req", "kv"),
        P("req", "kv"),
        P("req", "kv"),
        P("req", "kv"),
        P("req", None, "kv"),
        P("req", None, "kv"),
        P(),
        P(),
        P("kv", None),
        P("kv"),
        P(),
        P(),
        P("req", None, "kv"),
        P("req", None, "kv"),
        P("req", "kv", None),
    )
    return jax.shard_map(
        per_device, mesh=mesh, in_specs=in_specs, out_specs=P("req", "kv"), check_vma=False
    )
```

```python
import functools
import math

import jax
import jax.numpy as jnp
from jax import lax
from jax.experimental import pallas as pl
from jax.experimental.pallas import tpu as pltpu
from jax.sharding import PartitionSpec as P

MESH = pl.DeviceIdType.MESH
F32 = jnp.float32
BF16 = jnp.bfloat16

PART_TYPE = BF16
LAST_TYPE = BF16


def layer_kernel(
    n_req,
    n_kv,
    len_hbm,
    order_hbm,
    ids_hbm,
    gates_hbm,
    gain_hbm,
    res_hbm,
    q_hbm,
    k_hbm,
    v_hbm,
    keys_hbm,
    values_hbm,
    wo_hbm,
    wg_hbm,
    wu_hbm,
    wd_hbm,
    out_ref,
    rows,
    gains,
    keys,
    values,
    wo,
    wg,
    wu,
    wd,
    qmat,
    att,
    mine,
    part,
    normed,
    tokens,
    zsend,
    zrecv,
    in_sem,
    w_sem,
    kv_send,
    kv_recv,
    req_send,
    req_recv,
    z_sems,
    len_ref,
    order_ref,
    ids_ref,
    gates_ref,
    gain_ref,
    aux_sem,
):
    r = lax.axis_index("req")
    f = lax.axis_index("kv")
    per_dev, width = mine.shape
    q_width = q_hbm.shape[1]
    hd = k_hbm.shape[1]
    chunk = res_hbm.shape[1]
    heads = q_width // hd
    longest = keys.shape[1]
    total = n_req * per_dev

    def req_peer(d):
        return lax.rem(r + d, n_req)

    def kv_peer(k):
        return lax.rem(f + k, n_kv)

    barrier = pltpu.get_barrier_semaphore()
    for d in range(n_req - 1, 0, -1):
        pl.semaphore_signal(barrier, inc=1, device_id=(req_peer(d), f), device_id_type=MESH)
    for k in range(1, n_kv):
        pl.semaphore_signal(barrier, inc=1, device_id=(r, kv_peer(k)), device_id_type=MESH)

    places = (
        (q_hbm, 0, q_width),
        (k_hbm, q_width, hd),
        (v_hbm, q_width + hd, hd),
        (res_hbm, q_width + 2 * hd, chunk),
    )
    small = [
        pltpu.make_async_copy(src, rows.at[0, :, pl.ds(at, size)], in_sem.at[i])
        for i, (src, at, size) in enumerate(places)
    ]
    for c in small:
        c.start()
    gain_in = pltpu.make_async_copy(gain_hbm, gain_ref, aux_sem.at[0])
    aux = [
        pltpu.make_async_copy(src, dst, aux_sem.at[i])
        for i, (src, dst) in enumerate(
            (
                (len_hbm, len_ref),
                (order_hbm, order_ref),
                (ids_hbm, ids_ref),
                (gates_hbm, gates_ref),
            ),
            1,
        )
    ]
    for c in (gain_in, *aux):
        c.start()
    loads = []
    for i in range(per_dev):
        loads.append(pltpu.make_async_copy(keys_hbm.at[i], keys.at[i], w_sem.at[2 * i]))
        loads.append(pltpu.make_async_copy(values_hbm.at[i], values.at[i], w_sem.at[2 * i + 1]))
    base = 2 * per_dev
    load_wo = pltpu.make_async_copy(wo_hbm, wo, w_sem.at[base])
    load_wg = pltpu.make_async_copy(wg_hbm.at[0], wg, w_sem.at[base + 1])
    load_wu = pltpu.make_async_copy(wu_hbm.at[0], wu, w_sem.at[base + 2])
    load_wd = pltpu.make_async_copy(wd_hbm.at[0], wd, w_sem.at[base + 3])
    for c in loads:
        c.start()

    own_columns = pl.ds(pl.multiple_of(f * chunk, chunk), chunk)
    gain_in.wait()
    gains[:, own_columns] = gain_ref[...].astype(F32).reshape(1, -1)
    qmat[...] = jnp.zeros_like(qmat)
    att[...] = jnp.zeros_like(att)

    for c in small:
        c.wait()
    pl.semaphore_wait(barrier, n_req + n_kv - 2)

    def to_req(stage, d, src, dst):
        return pltpu.make_async_remote_copy(
            src_ref=src,
            dst_ref=dst,
            send_sem=req_send.at[stage, d],
            recv_sem=req_recv.at[stage, d],
            device_id=(req_peer(d), f),
            device_id_type=MESH,
        )

    def to_kv(stage, k, src, dst):
        return pltpu.make_async_remote_copy(
            src_ref=src,
            dst_ref=dst,
            send_sem=kv_send.at[stage, k],
            recv_sem=kv_recv.at[stage, k],
            device_id=(r, kv_peer(k)),
            device_id_type=MESH,
        )

    first = [to_req(0, d, rows.at[0], rows.at[d]) for d in range(1, n_req)]
    for c in first:
        c.start()
    own_gain = gains.at[:, own_columns]
    for c in (load_wo, load_wg, load_wu, load_wd):
        c.start()
    gain_out = [to_kv(0, k, own_gain, own_gain) for k in range(1, n_kv)]
    for c in gain_out:
        c.start()
    for c in (*aux, *loads, load_wo):
        c.wait()
    for c in first:
        c.wait_recv()

    inv_root = 1.0 / math.sqrt(hd)
    served = [order_ref[r * per_dev + i] for i in range(per_dev)]
    positions = lax.broadcasted_iota(jnp.int32, (1, longest), 1)
    residual, k_rows, v_rows = [], [], []
    for i in range(per_dev):
        t = served[i]
        src = t // per_dev
        pair = rows[lax.rem(r - src + n_req, n_req)].astype(F32)
        which = lax.broadcasted_iota(jnp.int32, pair.shape, 0) == t - src * per_dev
        row = jnp.sum(jnp.where(which, pair, 0.0), axis=0, keepdims=True)
        residual.append(row[:, q_width + 2 * hd :])
        k_rows.append(row[:, q_width : q_width + hd])
        v_rows.append(row[:, q_width + hd : q_width + 2 * hd])
        for h in range(heads):
            qmat[i, h : h + 1, :] = row[:, h * hd : (h + 1) * hd]
    ques = [qmat[i] for i in range(per_dev)]
    raw = [
        lax.dot_general(
            ques[i].astype(BF16), keys[i], (((1,), (1,)), ((), ())), preferred_element_type=F32
        )
        for i in range(per_dev)
    ]
    weights, own_weights, totals = [], [], []
    for i in range(per_dev):
        scores = jnp.where(positions < len_ref[served[i]], raw[i] * inv_root, -1e30)
        own = jnp.sum(ques[i] * k_rows[i], axis=1, keepdims=True) * inv_root
        highest = jnp.maximum(jnp.max(scores, axis=1, keepdims=True), own)
        w = jnp.exp(scores - highest)
        own_weight = jnp.exp(own - highest)
        totals.append(jnp.sum(w, axis=1, keepdims=True) + own_weight)
        weights.append(w.astype(BF16))
        own_weights.append(own_weight.astype(BF16).astype(F32))
    numerators = [
        jnp.dot(weights[i], values[i], preferred_element_type=F32) for i in range(per_dev)
    ]
    for i in range(per_dev):
        attended = (numerators[i] + own_weights[i] * v_rows[i]) / totals[i]
        for h in range(heads):
            att[i : i + 1, h * hd : (h + 1) * hd] = attended[h : h + 1, :]

    projected = jnp.dot(att[...].astype(BF16), wo[...], preferred_element_type=F32)
    mine[...] = projected[:per_dev]
    mine[:, own_columns] += jnp.concatenate(residual, axis=0)
    part[0] = mine[...].astype(part.dtype)
    second = [to_kv(1, k, part.at[0], part.at[k]) for k in range(1, n_kv)]
    for c in second:
        c.start()
    for c in gain_out:
        c.wait_recv()
    for c in second:
        c.wait_recv()
    hidden = mine[...]
    for k in range(1, n_kv):
        hidden = hidden + part[k].astype(F32)
    mine[...] = hidden
    squares = jnp.sum(hidden * hidden, axis=1, keepdims=True)
    normed[0] = (hidden * lax.rsqrt(squares / width + 1e-06) * gains[...]).astype(BF16)

    third = [to_req(1, d, normed.at[0], normed.at[d]) for d in range(1, n_req)]
    for c in third:
        c.start()

    gate_row = jnp.sum(jnp.where(ids_ref[...] == r, gates_ref[...], 0.0), axis=0, keepdims=True)
    token_of = lax.broadcasted_iota(jnp.int32, (total, total), 0)
    other_of = lax.broadcasted_iota(jnp.int32, (total, total), 1)
    gate = jnp.sum(jnp.where(token_of == other_of, gate_row, 0.0), axis=1, keepdims=True)
    slot_row = jnp.zeros((1, total), jnp.int32)
    slot_at = lax.broadcasted_iota(jnp.int32, (1, total), 1)
    for d in range(n_req):
        src = lax.rem(r - d + n_req, n_req)
        for i in range(per_dev):
            slot_row = jnp.where(
                slot_at == d * per_dev + i, order_ref[src * per_dev + i], slot_row
            )
    to_token = jnp.where(token_of == slot_row, 1.0, 0.0).astype(BF16)
    hidden_part = mine[:, own_columns]
    token_at = lax.broadcasted_iota(jnp.int32, (total, 1), 0)
    placed = jnp.zeros((total, chunk), F32)
    for i in range(per_dev):
        placed = placed + jnp.where(token_at == served[i], hidden_part[i : i + 1, :], 0.0)
    tokens[0:per_dev, :] = normed[0].astype(F32)
    load_wg.wait()
    load_wu.wait()
    load_wd.wait()

    for d, c in enumerate(third, 1):
        c.wait_recv()
        tokens[d * per_dev : (d + 1) * per_dev, :] = normed[d].astype(F32)
    x = tokens[...].astype(BF16)
    gate_h = jnp.dot(x, wg[...], preferred_element_type=F32)
    up_h = jnp.dot(x, wu[...], preferred_element_type=F32)
    inner = (gate_h / (1.0 + jnp.exp(-gate_h)) * up_h).astype(BF16)
    inner = jnp.dot(to_token, inner, preferred_element_type=F32).astype(BF16)

    fourth = []
    for k in (*range(1, n_kv), 0):
        columns = pl.ds(pl.multiple_of(kv_peer(k) * chunk, chunk), chunk)
        y = jnp.dot(inner, wd[:, columns], preferred_element_type=F32) * gate
        if k == 0:
            y = y + placed
        y = y.astype(zsend.dtype)
        for p in range(n_req):
            zsend[k, p] = y[p * per_dev : (p + 1) * per_dev, :]
        for d in range(n_req):
            if k == 0 and d == 0:
                continue
            c = pltpu.make_async_remote_copy(
                src_ref=zsend.at[k, req_peer(d)],
                dst_ref=zrecv.at[k, d],
                send_sem=z_sems.at[0, k * n_req + d],
                recv_sem=z_sems.at[1, k * n_req + d],
                device_id=(req_peer(d), kv_peer(k)),
                device_id_type=MESH,
            )
            c.start()
            fourth.append((k, d, c))
    z = zsend[0, r].astype(F32)
    for k, d, c in fourth:
        c.wait_recv()
        z = z + zrecv[k, d].astype(F32)
    out_ref[...] = z.astype(out_ref.dtype)
    for c in (*first, *gain_out, *second, *third):
        c.wait_send()
    for _, _, c in fourth:
        c.wait_send()


def per_device(
    residual_in,
    queries,
    fresh_token_keys,
    fresh_token_values,
    cached_key_slots,
    cached_value_slots,
    lengths,
    slot_order,
    out_proj,
    norm_gain,
    expert_ids,
    gate_values,
    gate_proj,
    up_proj,
    down_proj,
):
    n_req = lax.axis_size("req")
    n_kv = lax.axis_size("kv")
    per_dev, chunk = residual_in.shape
    q_width = queries.shape[1]
    hd = fresh_token_keys.shape[1]
    width = out_proj.shape[1]
    total = lengths.shape[0]
    row_width = q_width + 2 * hd + chunk
    heads_up = -(-(q_width // hd) // 8) * 8
    vmem = pl.BlockSpec(memory_space=pltpu.VMEM)
    hbm = pl.BlockSpec(memory_space=pl.ANY)
    return pl.pallas_call(
        functools.partial(layer_kernel, n_req, n_kv),
        out_shape=jax.ShapeDtypeStruct((per_dev, chunk), BF16),
        in_specs=[hbm] * 15,
        out_specs=vmem,
        scratch_shapes=[
            pltpu.VMEM((n_req, per_dev, row_width), BF16),
            pltpu.VMEM((1, width), F32),
            pltpu.VMEM(cached_key_slots.shape, BF16),
            pltpu.VMEM(cached_value_slots.shape, BF16),
            pltpu.VMEM(out_proj.shape, BF16),
            pltpu.VMEM(gate_proj.shape[1:], BF16),
            pltpu.VMEM(up_proj.shape[1:], BF16),
            pltpu.VMEM(down_proj.shape[1:], BF16),
            pltpu.VMEM((per_dev, heads_up, hd), F32),
            pltpu.VMEM((8, q_width), F32),
            pltpu.VMEM((per_dev, width), F32),
            pltpu.VMEM((n_kv, per_dev, width), PART_TYPE),
            pltpu.VMEM((n_req, per_dev, width), BF16),
            pltpu.VMEM((total, width), F32),
            pltpu.VMEM((n_kv, n_req, per_dev, chunk), LAST_TYPE),
            pltpu.VMEM((n_kv, n_req, per_dev, chunk), LAST_TYPE),
            pltpu.SemaphoreType.DMA((4,)),
            pltpu.SemaphoreType.DMA((2 * per_dev + 4,)),
            pltpu.SemaphoreType.DMA((2, n_kv)),
            pltpu.SemaphoreType.DMA((2, n_kv)),
            pltpu.SemaphoreType.DMA((2, n_req)),
            pltpu.SemaphoreType.DMA((2, n_req)),
            pltpu.SemaphoreType.DMA((2, n_kv * n_req)),
            pltpu.SMEM(lengths.shape, jnp.int32),
            pltpu.SMEM(slot_order.shape, jnp.int32),
            pltpu.VMEM(expert_ids.shape[::-1], jnp.int32),
            pltpu.VMEM(gate_values.shape[::-1], F32),
            pltpu.VMEM(norm_gain.shape, BF16),
            pltpu.SemaphoreType.DMA((5,)),
        ],
        compiler_params=pltpu.CompilerParams(
            collective_id=0, has_side_effects=True, vmem_limit_bytes=56 * 1024 * 1024
        ),
        cost_estimate=pl.CostEstimate(
            flops=400_000_000, bytes_accessed=14_000_000, transcendentals=100_000
        ),
    )(
        lengths,
        slot_order,
        expert_ids.T,
        gate_values.T,
        norm_gain,
        residual_in,
        queries,
        fresh_token_keys,
        fresh_token_values,
        cached_key_slots,
        cached_value_slots,
        out_proj,
        gate_proj,
        up_proj,
        down_proj,
    )


def solution(mesh):
    in_specs = (
        P("req", "kv"),
        P("req", "kv"),
        P("req", "kv"),
        P("req", "kv"),
        P("req", None, "kv"),
        P("req", None, "kv"),
        P(),
        P(),
        P("kv", None),
        P("kv"),
        P(),
        P(),
        P("req", None, "kv"),
        P("req", None, "kv"),
        P("req", "kv", None),
    )
    return jax.shard_map(
        per_device, mesh=mesh, in_specs=in_specs, out_specs=P("req", "kv"), check_vma=False
    )
```
